512 devices in a mesh: dp: 16 (over z), cell: 32 (over y, x, core).
Axes of the slice: x: 4, y: 4, z: 16, core: 2. Of those that a mesh axis runs over, the one named last changes fastest.
Arguments:
- counts: bfloat16 [16, 2048, 32768], P('dp', None, 'cell'), may hold values from 1 to 50
- shared: float32 [32, 2048], replicated, may hold values from 0.2 to 1.2
- view_factors: float32 [16, 32, 2048], P('dp'), may hold values from 0.2 to 1.2
- loadings: float32 [16, 32, 32768], P('dp', None, 'cell'), may hold values from 0.1 to 1
Outputs:
- shared_out: float32 [32, 2048], replicated
- views_out: float32 [16, 32, 2048], P('dp')
- loadings_out: float32 [16, 32, 32768], P('dp', None, 'cell')
The draws below stay inside these ranges and needn't reach their ends.
All inputs are finite; a program needn't handle non-finite values.
Results may differ from the reference program's by a relative error of at most 0.0004.
Values sent between devices are 32-bit elements; how exact they have to be, the bound alone decides.
A program may use at most 64 MiB of HBM per device.

```python
import math
import jax
import jax.numpy as jnp
from jax import lax

GENES = 2048
RANK = 32
ITERS = 3
OUTER_STEPS = 2
DATASETS = 16
CELLS = 32768


def level_of(stream_key, dims, cuts, low, top_value):
    level = 1.0
    for dim, blocks in cuts:
        heights = jax.random.uniform(jax.random.fold_in(jax.random.fold_in(stream_key, 6), dim), (blocks,), jnp.float32, low / len(cuts), top_value / len(cuts))
        level = level * jnp.repeat(jnp.exp(heights), dims[dim] // blocks).reshape((-1,) + (1,) * (len(dims) - 1 - dim))
    return level


def setup_inputs(seed: int = 0) -> dict:
    seeds = jax.random.split(jax.random.key(seed), 5)
    return {
        "counts": jnp.clip(jnp.exp(math.log(50.0) - 3.912023 * jax.random.uniform(seeds[0], (DATASETS, GENES, CELLS), jnp.float32) ** level_of(seeds[0], (DATASETS, GENES, CELLS), ((0, 16), (2, 32)), -0.2, 0.2)), 1.0, 50.0).astype(jnp.bfloat16),
        "shared": jnp.clip(jnp.exp(jax.random.uniform(seeds[1], (RANK, GENES), jnp.float32, math.log(0.2), math.log(1.2))), 0.2, 1.2),
        "view_factors": jnp.clip(jnp.exp(math.log(1.2) - 1.7917595 * jax.random.uniform(seeds[2], (DATASETS, RANK, GENES), jnp.float32) ** level_of(seeds[2], (DATASETS, RANK, GENES), ((0, 16),), -0.2, 0.2)), 0.2, 1.2),
        "loadings": jnp.clip(jnp.exp(math.log(1.0) - 2.3025851 * jax.random.uniform(seeds[3], (DATASETS, RANK, CELLS), jnp.float32) ** level_of(seeds[3], (DATASETS, RANK, CELLS), ((0, 16), (2, 32)), -0.2, 0.2)), 0.1, 1.0),
    }


penalty = 5.0


def highest(left, right):
    return jnp.dot(left, right, precision=lax.Precision.HIGHEST, preferred_element_type=jnp.float32)


def inner_updates(shared, view_factor, loading, matrix):
    for inner_index in range(ITERS):
        combined = shared + view_factor
        numerator = jnp.dot(combined.astype(jnp.bfloat16), matrix, preferred_element_type=jnp.float32)
        gramian = highest(combined, combined.T) + penalty * highest(view_factor, view_factor.T)
        loading = loading * numerator / highest(gramian, loading)
        rounded = loading.astype(jnp.bfloat16)
        crossed = lax.dot_general(rounded, matrix, (((1,), (1,)), ((), ())), preferred_element_type=jnp.float32)
        squared = highest(loading, loading.T)
        view_factor = view_factor * crossed / highest(squared, combined + penalty * view_factor)
    return view_factor, loading, crossed, squared


def reference(counts, shared, view_factors, loadings):
    for sweep_index in range(OUTER_STEPS):
        def per_set(triple):
            return inner_updates(shared, triple[0], triple[1], triple[2])

        view_factors, loadings, crossed, squared = lax.map(per_set, (view_factors, loadings, counts))
        totals = jnp.sum(crossed, axis=0)
        denominator = jnp.sum(jnp.einsum("ikl,ilg->ikg", squared, shared[None] + view_factors, precision=lax.Precision.HIGHEST), axis=0)
        shared = shared * totals / denominator
    return shared, view_factors, loadings
```

```python
import functools

import jax
import jax.numpy as jnp
from jax import lax
from jax.experimental import pallas as pl
from jax.experimental.pallas import tpu as pltpu
from jax.sharding import PartitionSpec as P

ITERS = 3
OUTER_STEPS = 2
PENALTY = 5.0

SIDE = 4
CHIPS = SIDE * SIDE
DEVICES = 2 * CHIPS
SETS = 16
RANK = 32
LANES = 128
ROWS = RANK // 2
HALF = ROWS // 2

f32, bf16 = jnp.float32, jnp.bfloat16
MESH = pl.DeviceIdType.MESH
NN = (((1,), (0,)), ((), ()))
NT = (((1,), (1,)), ((), ()))


def hops(d):
    return min(d, SIDE - d)


OFFSETS = sorted(
    ((dy, dx) for dy in range(SIDE) for dx in range(SIDE)),
    key=lambda o: (hops(o[0]) + hops(o[1]), o),
)
DISTANCE = [hops(dy) + hops(dx) for dy, dx in OFFSETS]
GROUPS = 5
GROUP_SIZE = [2 * DISTANCE.count(g) for g in range(GROUPS)]
GROUP_SIZE[0] = 1


def dot(a, b, dims=NN):
    return lax.dot_general(a, b, dims, preferred_element_type=f32)


def split(v):
    high = v.astype(bf16)
    return high, (v - high.astype(f32)).astype(bf16)


def kernel(
    x_hbm, w_hbm, v_hbm, h_hbm, w_out, v_out, h_out,
    x, w, v, h, n, z, parts, qsrc, pslots, qslots, m4, psum, qsum,
    zsrc, zpair, zhalf, zslots, wold,
    xsem, insem, outsem, psend, precv, qsend, qrecv, vsend, vrecv,
    z1send, z1recv, z2send, z2recv, z3send, z3recv, wsend, wrecv,
):
    dp = lax.axis_index("dp")
    me = lax.axis_index("cell")
    core = lax.rem(me, 2)
    chip = lax.div(me, 2)
    cy, cx = lax.div(chip, SIDE), lax.rem(chip, SIDE)
    parity = lax.rem(dp, 2)
    pair = dp + 1 - 2 * parity
    chips = [lax.rem(cy + dy, SIDE) * SIDE + lax.rem(cx + dx, SIDE) for dy, dx in OFFSETS]
    zothers = [lax.rem(dp + 2 * s, SETS) for s in range(1, SETS // 2)]

    def partners(i):
        if i == 0:
            return [(chip, 1 - core)]
        return [(chips[i], core), (chips[i], 1 - core)]

    def remote(src, dst, send, recv, where):
        return pltpu.make_async_remote_copy(
            src_ref=src, dst_ref=dst, send_sem=send, recv_sem=recv,
            device_id=where, device_id_type=MESH,
        )

    def settle(ref, send, recv):
        return remote(ref, ref, send, recv, {"cell": chip * 2 + 1 - core})

    barrier = pltpu.get_barrier_semaphore()
    count = 0
    for i in range(CHIPS):
        for c, k in partners(i):
            pl.semaphore_signal(barrier, inc=1, device_id={"cell": c * 2 + k}, device_id_type=MESH)
            count += 1
    for other in [pair] + zothers:
        pl.semaphore_signal(barrier, inc=1, device_id={"dp": other}, device_id_type=MESH)
        count += 1

    def load_h():
        return pltpu.make_async_copy(h_hbm, h, insem.at[2])

    def load_x(i):
        rows = pl.ds(pl.multiple_of(chips[i] * LANES, LANES), LANES)
        return pltpu.make_async_copy(x_hbm.at[rows], x.at[rows], xsem.at[i])

    def load_f(src, dst, c, s):
        return pltpu.make_async_copy(src.at[:, pl.ds(c * LANES, LANES)], dst.at[c], insem.at[s])

    for c in range(CHIPS):
        load_f(w_hbm, w, c, 0).start()
        load_f(v_hbm, v, c, 1).start()
    load_h().start()
    for i in range(CHIPS):
        load_x(i).start()
    pltpu.make_async_copy(w, w, insem.at[0]).wait()
    pltpu.make_async_copy(v, v, insem.at[1]).wait()

    def gather(i, c, first):
        vc = v[c]
        a = w[c] + vc
        ah, al = split(a)
        vh, vl = split(vc)
        s = jnp.concatenate([ah, al, vh, vl], axis=0)
        rows = pl.ds(pl.multiple_of(c * LANES, LANES), LANES)
        dn, dz = dot(ah, x[rows, :]), dot(s, s, NT)
        if first:
            n[...] = dn
            z[...] = dz
        else:
            n[...] += dn
            z[...] += dz

    for i in range(CHIPS):
        load_x(i).wait()
        gather(i, chips[i], i == 0)
    load_h().wait()
    pl.semaphore_wait(barrier, count)

    lane = lax.broadcasted_iota(jnp.int32, (RANK, LANES), 1)
    block = lane // RANK
    mine = pl.ds(pl.multiple_of(core * ROWS, ROWS), ROWS)

    def spread(m):
        high, low = split(m)
        return jnp.concatenate([jnp.concatenate([high, low], axis=1)] * 4, axis=0)

    def square_times(packed, right):
        both = jnp.concatenate([packed, packed], axis=0)
        row = lax.broadcasted_iota(jnp.int32, (ROWS, LANES), 0)
        keep = block[:ROWS] == 2 * core + row // 8
        high, low = split(jnp.where(keep, both, 0.0))
        r = dot(jnp.concatenate([high, low], axis=0), right)
        return (r[:ROWS, :LANES] + r[ROWS:, :LANES]) + (r[:ROWS, LANES:] + r[ROWS:, LANES:])

    def step(t, carry):
        zz = z[...]
        y = jnp.where(lane < 64, zz[:32] + zz[32:64], PENALTY * (zz[64:96] + zz[96:]))
        y = y + pltpu.roll(y, 64, 1)
        y = y + pltpu.roll(y, 32, 1)
        gh, gl = split(y)
        left = jnp.where(lane < 64, gh.astype(f32), gl.astype(f32)).astype(bf16)
        hv = h[...]
        hh, hl = split(hv)
        hv = hv * n[...] / dot(left, jnp.concatenate([hh, hl, hh, hl], axis=0))
        h[...] = hv
        hh, hl = split(hv)

        two = jnp.concatenate([hh, hl], axis=0)
        q = dot(two, jnp.concatenate([two, two], axis=0), NT)
        q = q[:32] + q[32:]
        q = q + pltpu.roll(q, 32, 1)
        q = jnp.where(block == lax.broadcasted_iota(jnp.int32, (RANK, LANES), 0) // 8, q, 0.0)
        packed = (q[0:8] + q[8:16]) + (q[16:24] + q[24:32])
        qsrc[...] = packed
        qslots[me] = packed
        for i in reversed(range(CHIPS)):
            for c, k in partners(i):
                remote(qsrc, qslots.at[me], qsend, qrecv, {"cell": c * 2 + k}).start()

        old = v[chip]
        shared = w[chip]
        wold[...] = shared
        m4[...] = spread(shared + old + PENALTY * old)

        for i in reversed(range(CHIPS)):
            c = chips[i]
            rows = pl.ds(pl.multiple_of(c * LANES, LANES), LANES)
            parts[c] = dot(hh, x[rows, :], NT)
            for c, k in partners(i):
                its = pl.ds(pl.multiple_of(k * ROWS, ROWS), ROWS)
                remote(parts.at[c, its], pslots.at[me], psend, precv, {"cell": c * 2 + k}).start()
        pslots[me] = parts[chip, mine]

        settle(qslots.at[pl.ds(0, DEVICES - 1)], qsend, qrecv).wait()
        qt = qslots[0]
        for i in range(1, DEVICES):
            qt = qt + qslots[i]
        qsum[...] = qt
        d = square_times(qt, m4[...])
        settle(pslots.at[pl.ds(0, DEVICES - 1)], psend, precv).wait()
        pt = pslots[0]
        for i in range(1, DEVICES):
            pt = pt + pslots[i]
        psum[...] = pt
        v[chip, mine] = v[chip, mine] * pt / d
        for i in reversed(range(CHIPS)):
            for c, k in partners(i):
                piece = v.at[chip, mine]
                remote(piece, piece, vsend, vrecv.at[DISTANCE[i]], {"cell": c * 2 + k}).start()

        def wait_v(g):
            settle(pslots.at[pl.ds(0, GROUP_SIZE[g])], vsend, vrecv.at[g]).wait_recv()

        wait_v(0)

        @pl.when(lax.rem(t, ITERS) == ITERS - 1)
        def _():
            d = square_times(qsum[...], spread(wold[...] + v[chip]))
            turn = lax.div(t, ITERS)
            for p in range(2):
                eight = pl.ds(p * HALF, HALF)
                zsrc[p, 0] = psum[eight, :]
                zsrc[p, 1] = d[p * HALF : (p + 1) * HALF]
            first = remote(zsrc.at[1 - parity], zpair, z1send, z1recv, {"dp": pair})
            first.start()
            first.wait()
            half = zsrc[parity] + zpair[...]
            zhalf[...] = half
            spot = lax.div(dp, 2)
            zslots[turn, spot] = half
            for other in zothers:
                remote(
                    zhalf, zslots.at[turn, spot], z2send.at[turn], z2recv.at[turn], {"dp": other}
                ).start()
            settle(zslots.at[turn, pl.ds(0, SETS // 2 - 1)], z2send.at[turn], z2recv.at[turn]).wait()
            total = zslots[turn, 0]
            for i in range(1, SETS // 2):
                total = total + zslots[turn, i]
            ours = pl.ds(pl.multiple_of(core * ROWS + parity * HALF, HALF), HALF)
            w[chip, ours] = w[chip, ours] * total[0] / total[1]
            piece = w.at[chip, ours]
            back = remote(piece, piece, z3send, z3recv, {"dp": pair})
            back.start()
            back.wait()
            for i in reversed(range(CHIPS)):
                for c, k in partners(i):
                    piece = w.at[chip, mine]
                    remote(piece, piece, wsend, wrecv, {"cell": c * 2 + k}).start()
            settle(pslots.at[pl.ds(0, DEVICES - 1)], wsend, wrecv).wait()

        @pl.when(t < ITERS * OUTER_STEPS - 1)
        def _():
            for i in range(CHIPS):
                if i and DISTANCE[i] != DISTANCE[i - 1]:
                    wait_v(DISTANCE[i])
                gather(i, chips[i], i == 0)

        @pl.when(t == ITERS * OUTER_STEPS - 1)
        def _():
            for g in range(1, GROUPS):
                wait_v(g)

        settle(pslots.at[pl.ds(0, DEVICES - 1)], vsend, vrecv.at[0]).wait_send()
        return carry

    lax.fori_loop(0, ITERS * OUTER_STEPS, step, 0)

    pltpu.make_async_copy(h, h_out, outsem.at[0]).start()
    for c in range(CHIPS):
        pltpu.make_async_copy(v.at[c], v_out.at[:, pl.ds(c * LANES, LANES)], outsem.at[1]).start()
        pltpu.make_async_copy(w.at[c], w_out.at[:, pl.ds(c * LANES, LANES)], outsem.at[2]).start()
    pltpu.make_async_copy(h, h_out, outsem.at[0]).wait()
    pltpu.make_async_copy(v, v, outsem.at[1]).wait()
    pltpu.make_async_copy(w, w, outsem.at[2]).wait()


def local(counts, shared, view_factors, loadings):
    genes, cells = counts.shape[1:]
    vmem = functools.partial(pltpu.VMEM, dtype=f32)
    dma = pltpu.SemaphoreType.DMA
    hbm = pl.BlockSpec(memory_space=pl.ANY)
    w, v, h = pl.pallas_call(
        kernel,
        out_shape=[
            jax.ShapeDtypeStruct((RANK, genes), f32),
            jax.ShapeDtypeStruct((RANK, genes), f32),
            jax.ShapeDtypeStruct((RANK, cells), f32),
        ],
        in_specs=[hbm] * 4,
        out_specs=[hbm] * 3,
        scratch_shapes=[
            pltpu.VMEM((genes, cells), bf16),
            vmem((CHIPS, RANK, LANES)),
            vmem((CHIPS, RANK, LANES)),
            vmem((RANK, cells)),
            vmem((RANK, cells)),
            vmem((LANES, LANES)),
            vmem((CHIPS, RANK, LANES)),
            vmem((8, LANES)),
            vmem((DEVICES, ROWS, LANES)),
            vmem((DEVICES, 8, LANES)),
            pltpu.VMEM((LANES, 2 * LANES), bf16),
            vmem((ROWS, LANES)),
            vmem((8, LANES)),
            vmem((2, 2, HALF, LANES)),
            vmem((2, HALF, LANES)),
            vmem((2, HALF, LANES)),
            vmem((OUTER_STEPS, SETS // 2, 2, HALF, LANES)),
            vmem((RANK, LANES)),
            dma((CHIPS,)), dma((3,)), dma((3,)),
            dma, dma, dma, dma, dma, dma((GROUPS,)),
            dma, dma, dma((OUTER_STEPS,)), dma((OUTER_STEPS,)), dma, dma, dma, dma,
        ],
        compiler_params=pltpu.CompilerParams(
            collective_id=0, has_side_effects=True, vmem_limit_bytes=40 * 2**20
        ),
    )(counts[0], shared, view_factors[0], loadings[0])
    return w, v[None], h[None]


def solution(mesh):
    in_specs = (P("dp", None, "cell"), P(), P("dp", None, None), P("dp", None, "cell"))
    out_specs = (P(), P("dp", None, None), P("dp", None, "cell"))
    return jax.shard_map(local, mesh=mesh, in_specs=in_specs, out_specs=out_specs, check_vma=False)
```

```python
import functools

import jax
import jax.numpy as jnp
from jax import lax
from jax.experimental import pallas as pl
from jax.experimental.pallas import tpu as pltpu
from jax.sharding import PartitionSpec as P

ITERS = 3
OUTER_STEPS = 2
PENALTY = 5.0

SIDE = 4
CHIPS = SIDE * SIDE
DEVICES = 2 * CHIPS
SETS = 16
RANK = 32
LANES = 128
ROWS = RANK // 2
HALF = ROWS // 2

f32, bf16 = jnp.float32, jnp.bfloat16
MESH = pl.DeviceIdType.MESH
NN = (((1,), (0,)), ((), ()))
NT = (((1,), (1,)), ((), ()))


def hops(d):
    return min(d, SIDE - d)


OFFSETS = sorted(
    ((dy, dx) for dy in range(SIDE) for dx in range(SIDE)),
    key=lambda o: (hops(o[0]) + hops(o[1]), o),
)
MIRROR = [OFFSETS.index((-dy % SIDE, -dx % SIDE)) for dy, dx in OFFSETS]


def dot(a, b, dims=NN):
    return lax.dot_general(a, b, dims, preferred_element_type=f32)


def split(v):
    high = v.astype(bf16)
    return high, (v - high.astype(f32)).astype(bf16)


def kernel(
    x_hbm, w_hbm, v_hbm, h_hbm, w_out, v_out, h_out,
    x, w, v, h, n, z, parts, qsrc, pslots, qslots, m4, qleft, wold,
    zsrc, zpair, zhalf, zslots, blank,
    xsem, insem, outsem, psend, precv, qsend, qrecv, vsend, vrecv,
    z1send, z1recv, z2send, z2recv, wsend, wrecv, hand,
):
    dp = lax.axis_index("dp")
    me = lax.axis_index("cell")
    core = lax.rem(me, 2)
    chip = lax.div(me, 2)
    cy, cx = lax.div(chip, SIDE), lax.rem(chip, SIDE)
    parity = lax.rem(dp, 2)
    pair = dp + 1 - 2 * parity
    chips = [lax.rem(cy + dy, SIDE) * SIDE + lax.rem(cx + dx, SIDE) for dy, dx in OFFSETS]
    zothers = [lax.rem(dp + 2 * s, SETS) for s in (4, 3, 5, 2, 6, 1, 7)]

    def along(s):
        return {"dp": lax.rem(dp + s + SETS, SETS)}

    def partners(i):
        if i == 0:
            return [(chip, 1 - core)]
        return [(chips[i], core), (chips[i], 1 - core)]

    def remote(src, dst, send, recv, where):
        return pltpu.make_async_remote_copy(
            src_ref=src, dst_ref=dst, send_sem=send, recv_sem=recv,
            device_id=where, device_id_type=MESH,
        )

    def settle(ref, send, recv):
        return remote(ref, ref, send, recv, {"cell": chip * 2 + 1 - core})

    barrier = pltpu.get_barrier_semaphore()
    count = 0
    for i in range(CHIPS):
        for c, k in partners(i):
            pl.semaphore_signal(barrier, inc=1, device_id={"cell": c * 2 + k}, device_id_type=MESH)
            count += 1
    for s in (-2, -1, 1, 2):
        pl.semaphore_signal(barrier, inc=1, device_id=along(s), device_id_type=MESH)
        count += 1

    def load_h():
        return pltpu.make_async_copy(h_hbm, h, insem.at[2])

    def load_x(i):
        rows = pl.ds(pl.multiple_of(chips[i] * LANES, LANES), LANES)
        return pltpu.make_async_copy(x_hbm.at[rows], x.at[rows], xsem.at[i])

    def load_f(src, dst, c, s):
        return pltpu.make_async_copy(src.at[:, pl.ds(c * LANES, LANES)], dst.at[c], insem.at[s])

    for c in range(CHIPS):
        load_f(w_hbm, w, c, 0).start()
        load_f(v_hbm, v, c, 1).start()
    load_h().start()
    for i in range(CHIPS):
        load_x(i).start()
    pltpu.make_async_copy(w, w, insem.at[0]).wait()
    pltpu.make_async_copy(v, v, insem.at[1]).wait()

    def gather(i, c, first):
        vc = v[c]
        a = w[c] + vc
        ah, al = split(a)
        vh, vl = split(vc)
        s = jnp.concatenate([ah, al, vh, vl], axis=0)
        rows = pl.ds(pl.multiple_of(c * LANES, LANES), LANES)
        dn, dz = dot(ah, x[rows, :]), dot(s, s, NT)
        if first:
            n[...] = dn
            z[...] = dz
        else:
            n[...] += dn
            z[...] += dz

    for i in range(CHIPS):
        load_x(i).wait()
        gather(i, chips[i], i == 0)
    load_h().wait()
    pl.semaphore_wait(barrier, count)

    for where in (along(-2), along(2), {"dp": pair}):
        pl.semaphore_signal(hand.at[0], inc=1, device_id=where, device_id_type=MESH)

    lane = lax.broadcasted_iota(jnp.int32, (RANK, LANES), 1)
    row = lax.broadcasted_iota(jnp.int32, (RANK, LANES), 0)
    block = lane // RANK
    mine = pl.ds(pl.multiple_of(core * ROWS, ROWS), ROWS)

    def spread(m):
        high, low = split(m)
        return jnp.concatenate([jnp.concatenate([high, low], axis=1)] * 4, axis=0)

    def square_times(left, right):
        r = dot(left, right)
        return (r[:ROWS, :LANES] + r[ROWS:, :LANES]) + (r[:ROWS, LANES:] + r[ROWS:, LANES:])

    def to_all(piece, send, recvs):
        for other in (1, 0):
            for i in reversed(range(CHIPS)):
                if other or i:
                    k = 1 - core if other else core
                    remote(piece, piece, send, recvs.at[MIRROR[i]], {"cell": chips[i] * 2 + k}).start()

    def wait_v(i):
        settle(pslots.at[pl.ds(0, 2 if i else 1)], vsend, vrecv.at[i]).wait_recv()

    def step(t, carry):
        zz = z[...]
        y = jnp.where(lane < 64, zz[:32] + zz[32:64], PENALTY * (zz[64:96] + zz[96:]))
        y = y + pltpu.roll(y, 64, 1)
        y = y + pltpu.roll(y, 32, 1)
        gh, gl = split(y)
        left = jnp.where(lane < 64, gh.astype(f32), gl.astype(f32)).astype(bf16)
        hv = h[...]
        hh, hl = split(hv)
        hv = hv * n[...] / dot(left, jnp.concatenate([hh, hl, hh, hl], axis=0))
        h[...] = hv
        hh, hl = split(hv)

        two = jnp.concatenate([hh, hl], axis=0)
        q = dot(two, jnp.concatenate([two, two], axis=0), NT)
        q = q[:32] + q[32:]
        q = q + pltpu.roll(q, 32, 1)
        q = jnp.where(block == lax.rem(row // 4, 4), q, 0.0)
        for k in range(2):
            packed = q[ROWS * k : ROWS * k + 8] + q[ROWS * k + 8 : ROWS * k + 16]
            packed = packed + pltpu.roll(packed, 4, 0)
            qsrc[k] = packed[:4]
        qslots[me] = qsrc[core]
        for i in reversed(range(CHIPS)):
            for c, k in partners(i):
                remote(qsrc.at[k], qslots.at[me], qsend, qrecv, {"cell": c * 2 + k}).start()

        old = v[chip]
        shared = w[chip]
        wold[...] = shared
        m4[...] = spread(shared + old + PENALTY * old)

        for i in reversed(range(CHIPS)):
            c = chips[i]
            rows = pl.ds(pl.multiple_of(c * LANES, LANES), LANES)
            parts[c] = dot(hh, x[rows, :], NT)
            for c, k in partners(i):
                its = pl.ds(pl.multiple_of(k * ROWS, ROWS), ROWS)
                remote(parts.at[c, its], pslots.at[me], psend, precv, {"cell": c * 2 + k}).start()
        pslots[me] = parts[chip, mine]

        settle(qslots.at[pl.ds(0, DEVICES - 1)], qsend, qrecv).wait()
        qt = qslots[0]
        for i in range(1, DEVICES):
            qt = qt + qslots[i]
        qt = jnp.where(block[:ROWS] == row[:ROWS] // 4, jnp.concatenate([qt] * 4, axis=0), 0.0)
        left = jnp.concatenate(split(qt), axis=0)
        qleft[...] = left
        d = square_times(left, m4[...])
        settle(pslots.at[pl.ds(0, DEVICES - 1)], psend, precv).wait()
        pt = pslots[0]
        for i in range(1, DEVICES):
            pt = pt + pslots[i]
        turn = lax.div(t, ITERS)
        last = lax.rem(t, ITERS) == ITERS - 1

        @pl.when(t == 0)
        def _():
            pl.semaphore_wait(hand.at[0], 3)
            for s in (-4, 4):
                pl.semaphore_signal(hand.at[1], inc=1, device_id=along(s), device_id_type=MESH)

        def to_pair(j):
            return remote(zsrc.at[j, 1 - parity], zpair.at[j], z1send.at[j], z1recv.at[j], {"dp": pair})

        def halve(j, total):
            zsrc[j, 0] = total[:HALF]
            zsrc[j, 1] = total[HALF:]
            to_pair(j).start()

        def to_others(j):
            to_pair(j).wait()
            half = zsrc[j, parity] + zpair[j]
            zhalf[j] = half
            spot = lax.div(dp, 2)
            zslots[turn, j, spot] = half
            for other in zothers:
                remote(
                    zhalf.at[j], zslots.at[turn, j, spot], z2send.at[turn, j], z2recv.at[turn, j], {"dp": other}
                ).start()

        def over_sets(j):
            settle(blank.at[pl.ds(0, SETS // 2 - 1)], z2send.at[turn, j], z2recv.at[turn, j]).wait()
            total = zslots[turn, j, 0]
            for i in range(1, SETS // 2):
                total = total + zslots[turn, j, i]
            return total

        @pl.when(last)
        def _():
            halve(0, pt)

        v[chip, mine] = v[chip, mine] * pt / d
        to_all(v.at[chip, mine], vsend, vrecv)
        wait_v(0)

        @pl.when(last)
        def _():
            halve(1, square_times(qleft[...], spread(wold[...] + v[chip])))

            @pl.when(turn == 0)
            def _():
                pl.semaphore_wait(hand.at[1], 2)

            to_others(0)
            to_others(1)

            @pl.when(turn == OUTER_STEPS - 1)
            def _():
                pltpu.make_async_copy(h, h_out, outsem.at[0]).start()
                for i in range(1, CHIPS):
                    wait_v(i)
                for c in range(CHIPS):
                    pltpu.make_async_copy(v.at[c], v_out.at[:, pl.ds(c * LANES, LANES)], outsem.at[1]).start()

            numerator = over_sets(0)
            denominator = over_sets(1)
            ours = pl.ds(pl.multiple_of(core * ROWS + parity * HALF, HALF), HALF)
            w[chip, ours] = w[chip, ours] * numerator / denominator
            piece = w.at[chip, ours]
            for i in reversed(range(CHIPS)):
                for z_to in (pair, dp):
                    for k in (1 - core, core):
                        if i or z_to is pair or k is not core:
                            remote(piece, piece, wsend, wrecv, {"dp": z_to, "cell": chips[i] * 2 + k}).start()
            settle(blank, wsend, wrecv).wait()

        @pl.when(t < ITERS * OUTER_STEPS - 1)
        def _():
            for i in range(CHIPS):
                if i:
                    wait_v(i)
                gather(i, chips[i], i == 0)

        settle(pslots.at[pl.ds(0, DEVICES - 1)], vsend, vrecv.at[0]).wait_send()
        return carry

    lax.fori_loop(0, ITERS * OUTER_STEPS, step, 0)

    for c in range(CHIPS):
        pltpu.make_async_copy(w.at[c], w_out.at[:, pl.ds(c * LANES, LANES)], outsem.at[2]).start()
    pltpu.make_async_copy(h, h_out, outsem.at[0]).wait()
    pltpu.make_async_copy(v, v, outsem.at[1]).wait()
    pltpu.make_async_copy(w, w, outsem.at[2]).wait()


def deliver(w, v, h, w_out, v_out, h_out, sem):
    copies = [
        pltpu.make_async_copy(src, dst, sem.at[i])
        for i, (src, dst) in enumerate([(w, w_out), (v, v_out), (h, h_out)])
    ]
    for copy in copies:
        copy.start()
    for copy in copies:
        copy.wait()


def local(counts, shared, view_factors, loadings):
    genes, cells = counts.shape[1:]
    vmem = functools.partial(pltpu.VMEM, dtype=f32)
    dma = pltpu.SemaphoreType.DMA
    hbm = pl.BlockSpec(memory_space=pl.ANY)
    w, v, h = pl.pallas_call(
        kernel,
        out_shape=[
            jax.ShapeDtypeStruct((RANK, genes), f32),
            jax.ShapeDtypeStruct((RANK, genes), f32),
            jax.ShapeDtypeStruct((RANK, cells), f32),
        ],
        in_specs=[hbm] * 4,
        out_specs=[hbm] * 3,
        scratch_shapes=[
            pltpu.VMEM((genes, cells), bf16),
            vmem((CHIPS, RANK, LANES)),
            vmem((CHIPS, RANK, LANES)),
            vmem((RANK, cells)),
            vmem((RANK, cells)),
            vmem((LANES, LANES)),
            vmem((CHIPS, RANK, LANES)),
            vmem((2, 4, LANES)),
            vmem((DEVICES, ROWS, LANES)),
            vmem((DEVICES, 4, LANES)),
            pltpu.VMEM((LANES, 2 * LANES), bf16),
            pltpu.VMEM((RANK, LANES), bf16),
            vmem((RANK, LANES)),
            vmem((2, 2, HALF, LANES)),
            vmem((2, HALF, LANES)),
            vmem((2, HALF, LANES)),
            vmem((OUTER_STEPS, 2, SETS // 2, HALF, LANES)),
            vmem((2 * DEVICES - 1, HALF, LANES)),
            dma((CHIPS,)), dma((3,)), dma((3,)),
            dma, dma, dma, dma, dma, dma((CHIPS,)),
            dma((2,)), dma((2,)), dma((OUTER_STEPS, 2)), dma((OUTER_STEPS, 2)), dma, dma,
            pltpu.SemaphoreType.REGULAR((2,)),
        ],
        compiler_params=pltpu.CompilerParams(
            collective_id=0, has_side_effects=True, vmem_limit_bytes=60 * 2**20
        ),
    )(counts[0], shared, view_factors[0], loadings[0])
    w, v, h = pl.pallas_call(
        deliver,
        out_shape=[jax.ShapeDtypeStruct(a.shape, f32) for a in (w, v, h)],
        in_specs=[pl.BlockSpec(memory_space=pltpu.VMEM)] * 3,
        out_specs=[hbm] * 3,
        scratch_shapes=[dma((3,))],
    )(w, v, h)
    return w, v[None], h[None]


def solution(mesh):
    in_specs = (P("dp", None, "cell"), P(), P("dp", None, None), P("dp", None, "cell"))
    out_specs = (P(), P("dp", None, None), P("dp", None, "cell"))
    return jax.shard_map(local, mesh=mesh, in_specs=in_specs, out_specs=out_specs, check_vma=False)
```

```python
import functools

import jax
import jax.numpy as jnp
from jax import lax
from jax.experimental import pallas as pl
from jax.experimental.pallas import tpu as pltpu
from jax.sharding import PartitionSpec as P

ITERS = 3
OUTER_STEPS = 2
PENALTY = 5.0

SIDE = 4
CHIPS = SIDE * SIDE
DEVICES = 2 * CHIPS
SETS = 16
RANK = 32
LANES = 128
ROWS = RANK // 2
HALF = ROWS // 2

f32, bf16 = jnp.float32, jnp.bfloat16
MESH = pl.DeviceIdType.MESH
NN = (((1,), (0,)), ((), ()))
NT = (((1,), (1,)), ((), ()))
TN = (((0,), (0,)), ((), ()))


def hops(d):
    return min(d, SIDE - d)


OFFSETS = sorted(
    ((dy, dx) for dy in range(SIDE) for dx in range(SIDE)),
    key=lambda o: (hops(o[0]) + hops(o[1]), o),
)
MIRROR = [OFFSETS.index((-dy % SIDE, -dx % SIDE)) for dy, dx in OFFSETS]


def dot(a, b, dims=NN):
    return lax.dot_general(a, b, dims, preferred_element_type=f32)


def split(v):
    high = v.astype(bf16)
    return high, (v - high.astype(f32)).astype(bf16)


def kernel(
    x_hbm, w_hbm, v_hbm, h_hbm, w_out, v_out, h_out,
    x, w, v, h, n, z, parts, qsrc, pslots, qslots, m4, qleft,
    psrc, ppair, dsrc, dslots, zhalf, zslots, blank,
    xsem, insem, outsem, psend, precv, qsend, qrecv, vsend, vrecv,
    z1send, z1recv, z2send, z2recv, wsend, wrecv, hand,
):
    dp = lax.axis_index("dp")
    me = lax.axis_index("cell")
    core = lax.rem(me, 2)
    chip = lax.div(me, 2)
    cy, cx = lax.div(chip, SIDE), lax.rem(chip, SIDE)
    parity = lax.rem(dp, 2)
    pair = dp + 1 - 2 * parity
    chips = [lax.rem(cy + dy, SIDE) * SIDE + lax.rem(cx + dx, SIDE) for dy, dx in OFFSETS]
    zothers = [lax.rem(dp + 2 * s, SETS) for s in (4, 3, 5, 2, 6, 1, 7)]

    def along(s):
        return {"dp": lax.rem(dp + s + SETS, SETS)}

    def partners(i):
        if i == 0:
            return [(chip, 1 - core)]
        return [(chips[i], core), (chips[i], 1 - core)]

    def remote(src, dst, send, recv, where):
        return pltpu.make_async_remote_copy(
            src_ref=src, dst_ref=dst, send_sem=send, recv_sem=recv,
            device_id=where, device_id_type=MESH,
        )

    def settle(ref, send, recv):
        return remote(ref, ref, send, recv, {"cell": chip * 2 + 1 - core})

    barrier = pltpu.get_barrier_semaphore()
    count = 0
    for i in range(CHIPS):
        for c, k in partners(i):
            pl.semaphore_signal(barrier, inc=1, device_id={"cell": c * 2 + k}, device_id_type=MESH)
            count += 1
    for s in (-2, -1, 1, 2):
        pl.semaphore_signal(barrier, inc=1, device_id=along(s), device_id_type=MESH)
        count += 1

    def load_h():
        return pltpu.make_async_copy(h_hbm, h, insem.at[2])

    def load_x(i):
        rows = pl.ds(pl.multiple_of(chips[i] * LANES, LANES), LANES)
        return pltpu.make_async_copy(x_hbm.at[rows], x.at[rows], xsem.at[i])

    def load_f(src, dst, c, s):
        return pltpu.make_async_copy(src.at[:, pl.ds(c * LANES, LANES)], dst.at[c], insem.at[s])

    for c in range(CHIPS):
        load_f(w_hbm, w, c, 0).start()
        load_f(v_hbm, v, c, 1).start()
    load_h().start()
    for i in range(CHIPS):
        load_x(i).start()
    pltpu.make_async_copy(w, w, insem.at[0]).wait()
    pltpu.make_async_copy(v, v, insem.at[1]).wait()

    def gather(batch):
        dn, dz, held = 0, 0, []
        for i in batch:
            c = chips[i]
            vc = v[c]
            a = w[c] + vc
            ah, al = split(a)
            vh, vl = split(vc)
            held.append(jnp.concatenate([ah, al, vh, vl], axis=0))
            rows = pl.ds(pl.multiple_of(c * LANES, LANES), LANES)
            dn = dn + dot(ah, x[rows, :])
        for j in range(0, len(held), 2):
            s = jnp.concatenate(held[j : j + 2], axis=1)
            dz = dz + dot(s, s, NT)
        if batch[0] == 0:
            n[...] = dn
            z[...] = dz
        else:
            n[...] += dn
            z[...] += dz

    groups = [range(0, 5), range(5, 11), range(11, 16)]
    for batch in groups:
        for i in batch:
            load_x(i).wait()
        gather(batch)
    load_h().wait()

    lane = lax.broadcasted_iota(jnp.int32, (RANK, LANES), 1)
    row = lax.broadcasted_iota(jnp.int32, (RANK, LANES), 0)
    block = lane // RANK
    mine = pl.ds(pl.multiple_of(core * ROWS, ROWS), ROWS)

    def spread(m):
        high, low = split(m)
        return jnp.concatenate([jnp.concatenate([high, low], axis=1)] * 4, axis=0)

    def square_times(left, right):
        r = dot(left, right)
        return (r[:ROWS, :LANES] + r[ROWS:, :LANES]) + (r[:ROWS, LANES:] + r[ROWS:, LANES:])

    def to_all(piece, send, recvs):
        for other in (1, 0):
            for i in reversed(range(CHIPS)):
                if other or i:
                    k = 1 - core if other else core
                    remote(piece, piece, send, recvs.at[MIRROR[i]], {"cell": chips[i] * 2 + k}).start()

    def wait_v(i):
        settle(pslots.at[pl.ds(0, 2 if i else 1)], vsend, vrecv.at[i]).wait_recv()

    def wait_w(i):
        settle(blank.at[pl.ds(0, 4 if i else 3)], wsend, wrecv.at[i]).wait_recv()

    def step(t, carry):
        zz = z[...]
        y = jnp.where(lane < 64, zz[:32] + zz[32:64], PENALTY * (zz[64:96] + zz[96:]))
        y = y + pltpu.roll(y, 64, 1)
        y = y + pltpu.roll(y, 32, 1)
        gh, gl = split(y)
        left = jnp.where(lane < 64, gh.astype(f32), gl.astype(f32)).astype(bf16)
        hv = h[...]
        hh, hl = split(hv)
        hv = hv * n[...] / dot(left, jnp.concatenate([hh, hl, hh, hl], axis=0))
        h[...] = hv
        hh, hl = split(hv)

        old = v[chip]
        m4[...] = spread(w[chip] + old + PENALTY * old)

        for batch in reversed(groups):
            for i in reversed(batch):
                rows = pl.ds(pl.multiple_of(chips[i] * LANES, LANES), LANES)
                parts[chips[i]] = dot(hh, x[rows, :], NT)
            if batch is groups[-1]:

                @pl.when(t < 1)
                def _():
                    pl.semaphore_wait(barrier, count)
                    for where in (along(-2), along(2), {"dp": pair}):
                        pl.semaphore_signal(hand.at[0], inc=1, device_id=where, device_id_type=MESH)

            for i in reversed(batch):
                for c, k in partners(i):
                    its = pl.ds(pl.multiple_of(k * ROWS, ROWS), ROWS)
                    remote(parts.at[c, its], pslots.at[me], psend, precv, {"cell": c * 2 + k}).start()
            if batch is groups[-1]:
                two = jnp.concatenate([hh, hl], axis=0)
                q = dot(two, jnp.concatenate([two, two], axis=0), NT)
                q = q[:32] + q[32:]
                q = q + pltpu.roll(q, 32, 1)
                q = jnp.where(block == lax.rem(row // 4, 4), q, 0.0)
                for k in range(2):
                    packed = q[ROWS * k : ROWS * k + 8] + q[ROWS * k + 8 : ROWS * k + 16]
                    packed = packed + pltpu.roll(packed, 4, 0)
                    qsrc[k] = packed[:4]
                qslots[me] = qsrc[core]
                for i in reversed(range(CHIPS)):
                    for c, k in partners(i):
                        remote(qsrc.at[k], qslots.at[me], qsend, qrecv, {"cell": c * 2 + k}).start()
        pslots[me] = parts[chip, mine]

        settle(qslots.at[pl.ds(0, DEVICES - 1)], qsend, qrecv).wait()
        qt = qslots[0]
        for i in range(1, DEVICES):
            qt = qt + qslots[i]
        qt = jnp.where(block[:ROWS] == row[:ROWS] // 4, jnp.concatenate([qt] * 4, axis=0), 0.0)
        left = jnp.concatenate(split(qt), axis=0)
        qleft[...] = left
        d = square_times(left, m4[...])
        settle(pslots.at[pl.ds(0, DEVICES - 1)], psend, precv).wait()
        pt = pslots[0]
        for i in range(1, DEVICES):
            pt = pt + pslots[i]
        turn = lax.div(t, ITERS)
        last = lax.rem(t, ITERS) == ITERS - 1

        @pl.when(t == 0)
        def _():
            pl.semaphore_wait(hand.at[0], 3)
            for s in (-4, 4):
                pl.semaphore_signal(hand.at[1], inc=1, device_id=along(s), device_id_type=MESH)

        def first_half():
            return remote(psrc.at[1 - parity], ppair, z1send.at[0], z1recv.at[0], {"dp": pair})

        def to_others(j, half):
            zhalf[j] = half
            spot = lax.div(dp, 2)
            zslots[turn, j, spot] = half
            for other in zothers:
                remote(
                    zhalf.at[j], zslots.at[turn, j, spot], z2send.at[turn, j], z2recv.at[turn, j], {"dp": other}
                ).start()

        def over_sets(j):
            settle(blank.at[pl.ds(0, SETS // 2 - 1)], z2send.at[turn, j], z2recv.at[turn, j]).wait()
            total = zslots[turn, j, 0]
            for i in range(1, SETS // 2):
                total = total + zslots[turn, j, i]
            return total

        @pl.when(last)
        def _():
            psrc[0] = pt[:HALF]
            psrc[1] = pt[HALF:]
            first_half().start()

        v[chip, mine] = v[chip, mine] * pt / d
        to_all(v.at[chip, mine], vsend, vrecv)

        @pl.when(last)
        def _():
            high, low = split(w[chip, mine] + v[chip, mine])
            e = dot(jnp.concatenate([qleft[...]] * 2, axis=0), jnp.concatenate([high, high, low, low], axis=0), TN)
            e = (e[:32] + e[32:64]) + (e[64:96] + e[96:])
            for k in range(2):
                for p in range(2):
                    dsrc[k, p] = e[ROWS * k + HALF * p : ROWS * k + HALF * (p + 1)]
            other = chip * 2 + 1 - core
            for spot, (k, p, where) in enumerate([
                (1 - core, 1 - parity, {"dp": pair, "cell": other}),
                (core, 1 - parity, {"dp": pair}),
                (1 - core, parity, {"cell": other}),
            ]):
                remote(dsrc.at[k, p], dslots.at[spot], z1send.at[1], z1recv.at[1], where).start()

            @pl.when(turn == 0)
            def _():
                pl.semaphore_wait(hand.at[1], 2)

            first_half().wait()
            to_others(0, psrc[parity] + ppair[...])
            settle(dslots, z1send.at[1], z1recv.at[1]).wait()
            to_others(1, (dsrc[core, parity] + dslots[0]) + (dslots[1] + dslots[2]))

            @pl.when(turn == OUTER_STEPS - 1)
            def _():
                pltpu.make_async_copy(h, h_out, outsem.at[0]).start()
                for i in range(CHIPS):
                    wait_v(i)
                for c in range(CHIPS):
                    pltpu.make_async_copy(v.at[c], v_out.at[:, pl.ds(c * LANES, LANES)], outsem.at[1]).start()

            numerator = over_sets(0)
            denominator = over_sets(1)
            ours = pl.ds(pl.multiple_of(core * ROWS + parity * HALF, HALF), HALF)
            w[chip, ours] = w[chip, ours] * numerator / denominator
            piece = w.at[chip, ours]
            for i in reversed(range(CHIPS)):
                for z_to in (pair, dp):
                    for k in (1 - core, core):
                        if i or z_to is pair or k is not core:
                            where = {"dp": z_to, "cell": chips[i] * 2 + k}
                            remote(piece, piece, wsend, wrecv.at[MIRROR[i]], where).start()

            @pl.when(turn == OUTER_STEPS - 1)
            def _():
                for i in range(CHIPS):
                    wait_w(i)

        @pl.when(t < ITERS * OUTER_STEPS - 1)
        def _():
            for batch in groups:
                for i in batch:
                    wait_v(i)

                @pl.when(last)
                def _():
                    for i in batch:
                        wait_w(i)

                gather(batch)

        settle(pslots.at[pl.ds(0, DEVICES - 1)], vsend, vrecv.at[0]).wait_send()

        @pl.when(last)
        def _():
            settle(blank, wsend, wrecv.at[0]).wait_send()

        return carry

    lax.fori_loop(0, ITERS * OUTER_STEPS, step, 0)

    for c in range(CHIPS):
        pltpu.make_async_copy(w.at[c], w_out.at[:, pl.ds(c * LANES, LANES)], outsem.at[2]).start()
    pltpu.make_async_copy(h, h_out, outsem.at[0]).wait()
    pltpu.make_async_copy(v, v, outsem.at[1]).wait()
    pltpu.make_async_copy(w, w, outsem.at[2]).wait()


def deliver(w, v, h, w_out, v_out, h_out, sem):
    copies = [
        pltpu.make_async_copy(src, dst, sem.at[i])
        for i, (src, dst) in enumerate([(w, w_out), (v, v_out), (h, h_out)])
    ]
    for copy in copies:
        copy.start()
    for copy in copies:
        copy.wait()


def local(counts, shared, view_factors, loadings):
    genes, cells = counts.shape[1:]
    vmem = functools.partial(pltpu.VMEM, dtype=f32)
    dma = pltpu.SemaphoreType.DMA
    hbm = pl.BlockSpec(memory_space=pl.ANY)
    w, v, h = pl.pallas_call(
        kernel,
        out_shape=[
            jax.ShapeDtypeStruct((RANK, genes), f32),
            jax.ShapeDtypeStruct((RANK, genes), f32),
            jax.ShapeDtypeStruct((RANK, cells), f32),
        ],
        in_specs=[hbm] * 4,
        out_specs=[hbm] * 3,
        scratch_shapes=[
            pltpu.VMEM((genes, cells), bf16),
            vmem((CHIPS, RANK, LANES)),
            vmem((CHIPS, RANK, LANES)),
            vmem((RANK, cells)),
            vmem((RANK, cells)),
            vmem((LANES, LANES)),
            vmem((CHIPS, RANK, LANES)),
            vmem((2, 4, LANES)),
            vmem((DEVICES, ROWS, LANES)),
            vmem((DEVICES, 4, LANES)),
            pltpu.VMEM((LANES, 2 * LANES), bf16),
            pltpu.VMEM((RANK, LANES), bf16),
            vmem((2, HALF, LANES)),
            vmem((HALF, LANES)),
            vmem((2, 2, HALF, LANES)),
            vmem((3, HALF, LANES)),
            vmem((2, HALF, LANES)),
            vmem((OUTER_STEPS, 2, SETS // 2, HALF, LANES)),
            vmem((2 * DEVICES - 1, HALF, LANES)),
            dma((CHIPS,)), dma((3,)), dma((3,)),
            dma, dma, dma, dma, dma, dma((CHIPS,)),
            dma((2,)), dma((2,)), dma((OUTER_STEPS, 2)), dma((OUTER_STEPS, 2)), dma, dma((CHIPS,)),
            pltpu.SemaphoreType.REGULAR((2,)),
        ],
        compiler_params=pltpu.CompilerParams(
            collective_id=0, has_side_effects=True, vmem_limit_bytes=60 * 2**20
        ),
    )(counts[0], shared, view_factors[0], loadings[0])
    w, v, h = pl.pallas_call(
        deliver,
        out_shape=[jax.ShapeDtypeStruct(a.shape, f32) for a in (w, v, h)],
        in_specs=[pl.BlockSpec(memory_space=pltpu.VMEM)] * 3,
        out_specs=[hbm] * 3,
        scratch_shapes=[dma((3,))],
    )(w, v, h)
    return w, v[None], h[None]


def solution(mesh):
    in_specs = (P("dp", None, "cell"), P(), P("dp", None, None), P("dp", None, "cell"))
    out_specs = (P(), P("dp", None, None), P("dp", None, "cell"))
    return jax.shard_map(local, mesh=mesh, in_specs=in_specs, out_specs=out_specs, check_vma=False)
```

```python
import functools

import jax
import jax.numpy as jnp
from jax import lax
from jax.experimental import pallas as pl
from jax.experimental.pallas import tpu as pltpu
from jax.sharding import PartitionSpec as P

ITERS = 3
OUTER_STEPS = 2
PENALTY = 5.0

SIDE = 4
CHIPS = SIDE * SIDE
DEVICES = 2 * CHIPS
SETS = 16
RANK = 32
LANES = 128
ROWS = RANK // 2
HALF = ROWS // 2

f32, bf16 = jnp.float32, jnp.bfloat16
MESH = pl.DeviceIdType.MESH
NN = (((1,), (0,)), ((), ()))
NT = (((1,), (1,)), ((), ()))
TN = (((0,), (0,)), ((), ()))


def hops(d):
    return min(d, SIDE - d)


OFFSETS = sorted(
    ((dy, dx) for dy in range(SIDE) for dx in range(SIDE)),
    key=lambda o: (hops(o[0]) + hops(o[1]), o),
)
MIRROR = [OFFSETS.index((-dy % SIDE, -dx % SIDE)) for dy, dx in OFFSETS]


def dot(a, b, dims=NN):
    return lax.dot_general(a, b, dims, preferred_element_type=f32)


def split(v):
    high = v.astype(bf16)
    return high, (v - high.astype(f32)).astype(bf16)


def kernel(
    x_hbm, w_hbm, v_hbm, h_hbm, w_out, v_out, h_out,
    x, w, v, h, n, z, parts, qsrc, pslots, qslots, m4, qleft,
    psrc, ppair, dsrc, dslots, zhalf, zslots, blank,
    xsem, insem, outsem, psend, precv, qsend, qrecv, vsend, vrecv,
    z1send, z1recv, z2send, z2recv, wsend, wrecv, hand,
):
    dp = lax.axis_index("dp")
    me = lax.axis_index("cell")
    core = lax.rem(me, 2)
    chip = lax.div(me, 2)
    cy, cx = lax.div(chip, SIDE), lax.rem(chip, SIDE)
    parity = lax.rem(dp, 2)
    pair = dp + 1 - 2 * parity
    chips = [lax.rem(cy + dy, SIDE) * SIDE + lax.rem(cx + dx, SIDE) for dy, dx in OFFSETS]
    zothers = [lax.rem(dp + 2 * s, SETS) for s in (4, 3, 5, 2, 6, 1, 7)]

    def along(s):
        return {"dp": lax.rem(dp + s + SETS, SETS)}

    def partners(i):
        if i == 0:
            return [(chip, 1 - core)]
        return [(chips[i], core), (chips[i], 1 - core)]

    def remote(src, dst, send, recv, where):
        return pltpu.make_async_remote_copy(
            src_ref=src, dst_ref=dst, send_sem=send, recv_sem=recv,
            device_id=where, device_id_type=MESH,
        )

    def settle(ref, send, recv):
        return remote(ref, ref, send, recv, {"cell": chip * 2 + 1 - core})

    barrier = pltpu.get_barrier_semaphore()
    count = 0
    for i in range(CHIPS):
        for c, k in partners(i):
            pl.semaphore_signal(barrier, inc=1, device_id={"cell": c * 2 + k}, device_id_type=MESH)
            count += 1
    for s in (-2, -1, 1, 2):
        pl.semaphore_signal(barrier, inc=1, device_id=along(s), device_id_type=MESH)
        count += 1

    def load_h():
        return pltpu.make_async_copy(h_hbm, h, insem.at[2])

    def load_x(i):
        rows = pl.ds(pl.multiple_of(chips[i] * LANES, LANES), LANES)
        return pltpu.make_async_copy(x_hbm.at[rows], x.at[rows], xsem.at[i])

    def load_f(src, dst, c, s):
        return pltpu.make_async_copy(src.at[:, pl.ds(c * LANES, LANES)], dst.at[c], insem.at[s])

    for c in range(CHIPS):
        load_f(w_hbm, w, c, 0).start()
        load_f(v_hbm, v, c, 1).start()
    load_h().start()
    for i in range(CHIPS):
        load_x(i).start()
    pltpu.make_async_copy(w, w, insem.at[0]).wait()
    pltpu.make_async_copy(v, v, insem.at[1]).wait()

    def gather(batch):
        dn, dz, held = 0, 0, []
        for i in batch:
            c = chips[i]
            vc = v[c]
            a = w[c] + vc
            ah, al = split(a)
            vh, vl = split(vc)
            held.append(jnp.concatenate([ah, al, vh, vl], axis=0))
            rows = pl.ds(pl.multiple_of(c * LANES, LANES), LANES)
            dn = dn + dot(ah, x[rows, :])
        for j in range(0, len(held), 2):
            s = jnp.concatenate(held[j : j + 2], axis=1)
            dz = dz + dot(s, s, NT)
        if batch[0] == 0:
            n[...] = dn
            z[...] = dz
        else:
            n[...] += dn
            z[...] += dz

    groups = [range(0, 5), range(5, 11), range(11, 16)]
    for batch in groups:
        for i in batch:
            load_x(i).wait()
        gather(batch)
    load_h().wait()

    lane = lax.broadcasted_iota(jnp.int32, (RANK, LANES), 1)
    row = lax.broadcasted_iota(jnp.int32, (RANK, LANES), 0)
    block = lane // RANK
    mine = pl.ds(pl.multiple_of(core * ROWS, ROWS), ROWS)

    def spread(m):
        high, low = split(m)
        return jnp.concatenate([jnp.concatenate([high, low], axis=1)] * 4, axis=0)

    def square_times(left, right):
        r = dot(left, right)
        return (r[:ROWS, :LANES] + r[ROWS:, :LANES]) + (r[:ROWS, LANES:] + r[ROWS:, LANES:])

    def to_all(piece, send, recvs):
        for other in (1, 0):
            for i in reversed(range(CHIPS)):
                if other or i:
                    k = 1 - core if other else core
                    remote(piece, piece, send, recvs.at[MIRROR[i]], {"cell": chips[i] * 2 + k}).start()

    def wait_v(i):
        settle(pslots.at[pl.ds(0, 2 if i else 1)], vsend, vrecv.at[i]).wait_recv()

    def wait_w(i):
        settle(blank.at[pl.ds(0, 4 if i else 3)], wsend, wrecv.at[i]).wait_recv()

    def step(t, carry):
        zz = z[...]
        y = jnp.where(lane < 64, zz[:32] + zz[32:64], PENALTY * (zz[64:96] + zz[96:]))
        y = y + pltpu.roll(y, 64, 1)
        y = y + pltpu.roll(y, 32, 1)
        gh, gl = split(y)
        left = jnp.where(lane < 64, gh.astype(f32), gl.astype(f32)).astype(bf16)
        hv = h[...]
        hh, hl = split(hv)
        hv = hv * n[...] / dot(left, jnp.concatenate([hh, hl, hh, hl], axis=0))
        h[...] = hv
        hh, hl = split(hv)

        old = v[chip]
        m4[...] = spread(w[chip] + old + PENALTY * old)

        for batch in reversed(groups):
            for i in reversed(batch):
                rows = pl.ds(pl.multiple_of(chips[i] * LANES, LANES), LANES)
                parts[chips[i]] = dot(hh, x[rows, :], NT)
            if batch is groups[-1]:

                @pl.when(t < 1)
                def _():
                    pl.semaphore_wait(barrier, count)
                    for where in (along(-2), along(-1), along(1), along(2)):
                        pl.semaphore_signal(hand.at[0], inc=1, device_id=where, device_id_type=MESH)

            for other in (1, 0):
                for i in reversed(batch):
                    if not (other or i):
                        continue
                    c, k = chips[i], 1 - core if other else core
                    its = pl.ds(pl.multiple_of(k * ROWS, ROWS), ROWS)
                    remote(parts.at[c, its], pslots.at[me], psend, precv, {"cell": c * 2 + k}).start()
            if batch is groups[-1]:
                two = jnp.concatenate([hh, hl], axis=0)
                q = dot(two, jnp.concatenate([two, two], axis=0), NT)
                q = q[:32] + q[32:]
                q = q + pltpu.roll(q, 32, 1)
                q = jnp.where(block == lax.rem(row // 4, 4), q, 0.0)
                for k in range(2):
                    packed = q[ROWS * k : ROWS * k + 8] + q[ROWS * k + 8 : ROWS * k + 16]
                    packed = packed + pltpu.roll(packed, 4, 0)
                    qsrc[k] = packed[:4]
                qslots[me] = qsrc[core]
                for i, other in [(i, other) for other in (1, 0) for i in reversed(range(CHIPS)) if i or other]:
                    for c, k in [(chips[i], 1 - core if other else core)]:
                        remote(qsrc.at[k], qslots.at[me], qsend, qrecv, {"cell": c * 2 + k}).start()
        pslots[me] = parts[chip, mine]

        settle(qslots.at[pl.ds(0, DEVICES - 1)], qsend, qrecv).wait()
        qt = qslots[0]
        for i in range(1, DEVICES):
            qt = qt + qslots[i]
        qt = jnp.where(block[:ROWS] == row[:ROWS] // 4, jnp.concatenate([qt] * 4, axis=0), 0.0)
        left = jnp.concatenate(split(qt), axis=0)
        qleft[...] = left
        ratio = v[chip, mine] / square_times(left, m4[...])
        settle(pslots.at[pl.ds(0, DEVICES - 1)], psend, precv).wait()
        pt = [pslots[i] for i in range(DEVICES)]
        while len(pt) > 1:
            pt = [a + b for a, b in zip(pt[::2], pt[1::2])]
        pt = pt[0]
        turn = lax.div(t, ITERS)
        last = lax.rem(t, ITERS) == ITERS - 1

        def first_half():
            return remote(psrc.at[1 - parity], ppair, z1send.at[0], z1recv.at[0], {"dp": pair})

        def to_others(j, half):
            zhalf[j] = half
            spot = lax.div(dp, 2)
            zslots[turn, j, spot] = half
            for other in zothers:
                remote(
                    zhalf.at[j], zslots.at[turn, j, spot], z2send.at[turn, j], z2recv.at[turn, j], {"dp": other}
                ).start()

        def over_sets(j):
            settle(blank.at[pl.ds(0, SETS // 2 - 1)], z2send.at[turn, j], z2recv.at[turn, j]).wait()
            total = zslots[turn, j, 0]
            for i in range(1, SETS // 2):
                total = total + zslots[turn, j, i]
            return total

        v[chip, mine] = pt * ratio
        to_all(v.at[chip, mine], vsend, vrecv)
        psrc[0] = pt[:HALF]
        psrc[1] = pt[HALF:]

        @pl.when(t == 0)
        def _():
            pl.semaphore_wait(hand.at[0], 4)
            for s in (-4, 4):
                pl.semaphore_signal(hand.at[1], inc=1, device_id=along(s), device_id_type=MESH)

        @pl.when(last)
        def _():
            first_half().start()
            high, low = split(w[chip, mine] + v[chip, mine])
            e = dot(jnp.concatenate([qleft[...]] * 2, axis=0), jnp.concatenate([high, high, low, low], axis=0), TN)
            e = (e[:32] + e[32:64]) + (e[64:96] + e[96:])
            for k in range(2):
                for p in range(2):
                    dsrc[k, p] = e[ROWS * k + HALF * p : ROWS * k + HALF * (p + 1)]
            other = chip * 2 + 1 - core
            for spot, (k, p, where) in enumerate([
                (1 - core, 1 - parity, {"dp": pair, "cell": other}),
                (core, 1 - parity, {"dp": pair}),
                (1 - core, parity, {"cell": other}),
            ]):
                remote(dsrc.at[k, p], dslots.at[spot], z1send.at[1], z1recv.at[1], where).start()

            @pl.when(turn == 0)
            def _():
                pl.semaphore_wait(hand.at[1], 2)

            first_half().wait()
            to_others(0, psrc[parity] + ppair[...])
            settle(dslots, z1send.at[1], z1recv.at[1]).wait()
            to_others(1, (dsrc[core, parity] + dslots[0]) + (dslots[1] + dslots[2]))

            @pl.when(turn == OUTER_STEPS - 1)
            def _():
                pltpu.make_async_copy(h, h_out, outsem.at[0]).start()
                for i in range(CHIPS):
                    wait_v(i)
                for c in range(CHIPS):
                    pltpu.make_async_copy(v.at[c], v_out.at[:, pl.ds(c * LANES, LANES)], outsem.at[1]).start()

            numerator = over_sets(0)
            denominator = over_sets(1)
            ours = pl.ds(pl.multiple_of(core * ROWS + parity * HALF, HALF), HALF)
            w[chip, ours] = w[chip, ours] * numerator / denominator
            piece = w.at[chip, ours]
            for i in reversed(range(CHIPS)):
                for z_to, k in ((along(1), core), (along(-1), 1 - core), ({}, 1 - core), ({}, core)):
                    if i or z_to or k is not core:
                        where = {"cell": chips[i] * 2 + k, **z_to}
                        remote(piece, piece, wsend, wrecv.at[MIRROR[i]], where).start()

            @pl.when(turn == OUTER_STEPS - 1)
            def _():
                for i in range(CHIPS):
                    wait_w(i)
                    genes = pl.ds(pl.multiple_of(chips[i] * LANES, LANES), LANES)
                    pltpu.make_async_copy(w.at[chips[i]], w_out.at[:, genes], outsem.at[2]).start()

        @pl.when(t < ITERS * OUTER_STEPS - 1)
        def _():
            for batch in (groups[0], groups[2], groups[1]):
                for i in batch:
                    wait_v(i)

                @pl.when(last)
                def _():
                    for i in batch:
                        wait_w(i)

                gather(batch)

        settle(pslots.at[pl.ds(0, DEVICES - 1)], vsend, vrecv.at[0]).wait_send()

        @pl.when(last)
        def _():
            settle(blank, wsend, wrecv.at[0]).wait_send()

        return carry

    lax.fori_loop(0, ITERS * OUTER_STEPS, step, 0)

    pltpu.make_async_copy(h, h_out, outsem.at[0]).wait()
    pltpu.make_async_copy(v, v, outsem.at[1]).wait()
    pltpu.make_async_copy(w, w, outsem.at[2]).wait()


def deliver(w, v, h, w_out, v_out, h_out, sem):
    copies = [
        pltpu.make_async_copy(src, dst, sem.at[i])
        for i, (src, dst) in enumerate([(w, w_out), (v, v_out), (h, h_out)])
    ]
    for copy in copies:
        copy.start()
    for copy in copies:
        copy.wait()


def local(counts, shared, view_factors, loadings):
    genes, cells = counts.shape[1:]
    vmem = functools.partial(pltpu.VMEM, dtype=f32)
    dma = pltpu.SemaphoreType.DMA
    hbm = pl.BlockSpec(memory_space=pl.ANY)
    w, v, h = pl.pallas_call(
        kernel,
        out_shape=[
            jax.ShapeDtypeStruct((RANK, genes), f32),
            jax.ShapeDtypeStruct((RANK, genes), f32),
            jax.ShapeDtypeStruct((RANK, cells), f32),
        ],
        in_specs=[hbm] * 4,
        out_specs=[hbm] * 3,
        scratch_shapes=[
            pltpu.VMEM((genes, cells), bf16),
            vmem((CHIPS, RANK, LANES)),
            vmem((CHIPS, RANK, LANES)),
            vmem((RANK, cells)),
            vmem((RANK, cells)),
            vmem((LANES, LANES)),
            vmem((CHIPS, RANK, LANES)),
            vmem((2, 4, LANES)),
            vmem((DEVICES, ROWS, LANES)),
            vmem((DEVICES, 4, LANES)),
            pltpu.VMEM((LANES, 2 * LANES), bf16),
            pltpu.VMEM((RANK, LANES), bf16),
            vmem((2, HALF, LANES)),
            vmem((HALF, LANES)),
            vmem((2, 2, HALF, LANES)),
            vmem((3, HALF, LANES)),
            vmem((2, HALF, LANES)),
            vmem((OUTER_STEPS, 2, SETS // 2, HALF, LANES)),
            vmem((2 * DEVICES - 1, HALF, LANES)),
            dma((CHIPS,)), dma((3,)), dma((3,)),
            dma, dma, dma, dma, dma, dma((CHIPS,)),
            dma((2,)), dma((2,)), dma((OUTER_STEPS, 2)), dma((OUTER_STEPS, 2)), dma, dma((CHIPS,)),
            pltpu.SemaphoreType.REGULAR((2,)),
        ],
        compiler_params=pltpu.CompilerParams(
            collective_id=0, has_side_effects=True, vmem_limit_bytes=60 * 2**20
        ),
    )(counts[0], shared, view_factors[0], loadings[0])
    w, v, h = pl.pallas_call(
        deliver,
        out_shape=[jax.ShapeDtypeStruct(a.shape, f32) for a in (w, v, h)],
        in_specs=[pl.BlockSpec(memory_space=pltpu.VMEM)] * 3,
        out_specs=[hbm] * 3,
        scratch_shapes=[dma((3,))],
    )(w, v, h)
    return w, v[None], h[None]


def solution(mesh):
    in_specs = (P("dp", None, "cell"), P(), P("dp", None, None), P("dp", None, "cell"))
    out_specs = (P(), P("dp", None, None), P("dp", None, "cell"))
    return jax.shard_map(local, mesh=mesh, in_specs=in_specs, out_specs=out_specs, check_vma=False)
```
